32 devices in a mesh: groups: 2 (over x), ctx: 8 (over z, y), rep: 2 (over core).
Axes of the slice: x: 2, y: 2, z: 4, core: 2. Of those that a mesh axis runs over, the one named last changes fastest.
Arguments:
- queries: bfloat16 [256, 16, 128], P(('groups', 'ctx', 'rep')), parts along dimension 0, may hold values from -40 to 40
- cache: bfloat16 [2, 2, 65536, 128], P('rep', None, ('groups', 'ctx')), parts along dimension 2, may hold values from -4 to 4
- owner: int32 [16], P(('groups', 'ctx')), parts along dimension 0, may hold values from 0 to 1
- lengths: int32 [256], P(('groups', 'ctx', 'rep')), parts along dimension 0, may hold values from 2 to 32768, as said below
Outputs:
- attended: bfloat16 [256, 16, 128], P(('groups', 'ctx', 'rep')), parts along dimension 0
The draws below stay inside these ranges and needn't reach their ends.
There are 2 independent parts, one for each index of `groups`. The reference program is written for one: setup_inputs(seed, part) draws one part's arguments, and reference() takes and returns one part's arrays. A program takes and returns all parts, laid end to end along the dimension named above; each array names one. Nothing has to cross between parts.
Inputs may be any that keep to these rules, and one draw needn't show every extreme that they name: `lengths`: some request in every draw uses the whole prefix.
All inputs are finite; a program needn't handle non-finite values.
Results may differ from the reference program's by a relative error of at most 0.003.
Values may be sent and summed in bfloat16 or wider, within the bound.
A program may use at most 64 MiB of HBM per device.

```python
import jax
import jax.numpy as jnp
from jax import lax

HEADS = 16
HD = 128
S_DEV = 4096
PREFIX = 32768
REQS = 128
N_CTX = 8
N_REP = 2


def draw_cache(key, part):
    shape = (N_REP, 2, PREFIX, HD)
    filled = jnp.clip(jax.random.normal(jax.random.fold_in(key, 1), shape, jnp.float32), -4.0, 4.0)
    return filled.astype(jnp.bfloat16)


def draw_queries(key, part):
    shape = (REQS, HEADS, HD)
    filled = jnp.clip(3.0 * jax.random.normal(jax.random.fold_in(key, 2), shape, jnp.float32), -12.0, 12.0)
    return filled.astype(jnp.bfloat16)


def draw_lengths(key, part):
    drawn = jax.random.randint(jax.random.fold_in(key, 3), (REQS,), 2, PREFIX + 1)
    return drawn.at[0].set(PREFIX).astype(jnp.int32)


def place_ends(result, stream_key, least, top_value):
    longest = result.shape.index(max(result.shape))
    spots = []
    for shift in (0, 1):
        where = [jax.random.randint(jax.random.fold_in(stream_key, axis), (), 0, length) for axis, length in enumerate(result.shape)]
        where[longest] = (where[longest] + shift) % result.shape[longest]
        spots.append(tuple(where))
    return result.at[spots[0]].set(least).at[spots[1]].set(top_value)


def setup_inputs(seed: int = 0, part: int = 0) -> dict:
    key_list = jax.random.split(jax.random.key(seed), 5)
    own_keys = jax.random.split(jax.random.fold_in(key_list[4], part), 5)
    return {
        "queries": draw_queries(jax.random.fold_in(jax.random.fold_in(key_list[4], part), 71), part),
        "cache": draw_cache(jax.random.fold_in(jax.random.fold_in(key_list[4], part), 71), part),
        "owner": place_ends(jax.random.randint(own_keys[2], (N_CTX,), 0, N_REP), jax.random.fold_in(own_keys[2], 1), 0, N_REP - 1).astype(jnp.int32),
        "lengths": draw_lengths(jax.random.fold_in(jax.random.fold_in(key_list[4], part), 71), part),
    }


def shard_partials(query_rows, row_lens, keys, values, start):
    scores = lax.dot_general(query_rows, keys, (((1,), (1,)), ((), ())), preferred_element_type=jnp.float32)
    scores = scores * (keys.shape[1] ** -0.5)
    positions = start + jnp.arange(keys.shape[0], dtype=jnp.int32)
    valid = positions[None, :] < row_lens[:, None]
    masked = jnp.where(valid, scores, jnp.float32(-1e30))
    top = jnp.max(masked, axis=1)
    weights = jnp.where(valid, jnp.exp(masked - top[:, None]), jnp.float32(0.0)).astype(jnp.bfloat16)
    total = jnp.sum(weights.astype(jnp.float32), axis=1)
    partial_value = jnp.dot(weights, values, preferred_element_type=jnp.float32)
    return top, total, partial_value


def combine(first, second):
    top = jnp.maximum(first[0], second[0])
    scale_a = jnp.exp(first[0] - top)
    scale_b = jnp.exp(second[0] - top)
    total = first[1] * scale_a + second[1] * scale_b
    partial_value = first[2] * scale_a[:, None] + second[2] * scale_b[:, None]
    return top, total, partial_value


def reference(queries, cache, owner, lengths):
    rows = REQS * HEADS
    query_rows = queries.reshape(rows, HD)
    row_lens = jnp.repeat(lengths, HEADS)

    def step(carry, shard):
        slot = owner[shard].astype(jnp.int32)
        start = (shard * S_DEV).astype(jnp.int32)
        zero = jnp.zeros((), jnp.int32)
        block = lax.dynamic_slice(cache, (slot, zero, start, zero), (1, 2, S_DEV, HD))[0]
        part = shard_partials(query_rows, row_lens, block[0], block[1], start)
        return combine(carry, part), None

    init = (jnp.full((rows,), -1e30, jnp.float32), jnp.zeros((rows,), jnp.float32), jnp.zeros((rows, HD), jnp.float32))
    (top, total, partial_value), _ = lax.scan(step, init, jnp.arange(N_CTX, dtype=jnp.int32))
    return (partial_value / total[:, None]).astype(jnp.bfloat16).reshape(REQS, HEADS, HD)
```

```python
import functools
import math

import jax
import jax.numpy as jnp
from jax import lax
from jax.experimental import pallas as pl
from jax.experimental.pallas import tpu as pltpu
from jax.sharding import PartitionSpec as P

MESH = pl.DeviceIdType.MESH
KEYS = 256
DEPTH = 1024


def distance(slot, count):
    return count // 2 + (1 - 2 * (slot % 2)) * ((slot + 1) // 2)


def kernel(
    count, heads, pack,
    q_ref, cache_ref, owner_ref, len_ref, out_ref,
    own_kv, got_kv, k_buf, v_buf, q_buf, len_buf, len_out, s_buf, snd, rcv,
    kv_send, kv_recv, kv_local, q_send, q_recv, l_send, l_recv, o_send, o_recv,
):
    me = lax.axis_index("ctx")
    rep = lax.axis_index("rep")
    rows, width = q_ref.shape
    reqs = rows // heads
    span = cache_ref.shape[2]
    factor = width ** (-0.5) * math.log2(math.e)
    other = 1 - rep

    locals_ = [
        pltpu.make_async_copy(cache_ref.at[0, i], own_kv.at[i], kv_local.at[i]) for i in range(2)
    ]
    for copy in locals_:
        copy.start()

    barrier = pltpu.get_barrier_semaphore()
    for t in range(1, count):
        pl.semaphore_signal(
            barrier, inc=1, device_id={"ctx": (me + t) % count}, device_id_type=MESH
        )
    pl.semaphore_signal(barrier, inc=1, device_id={"rep": other}, device_id_type=MESH)

    for i in range(reqs):
        len_out[i : i + 1, :] = jnp.full((1, 128), len_ref[i], jnp.int32)
    len_buf[count - 1] = len_out[...]
    q_buf[count - 1] = q_ref[...]
    v_buf[:, width:] = jnp.ones((span, width), jnp.bfloat16)
    pl.semaphore_wait(barrier, count)

    kv = [
        pltpu.make_async_remote_copy(
            src_ref=cache_ref.at[0, i], dst_ref=got_kv.at[i],
            send_sem=kv_send.at[i], recv_sem=kv_recv.at[i],
            device_id={"rep": other}, device_id_type=MESH,
        )
        for i in range(2)
    ]
    qs, ls = [], []
    for j in range(count - 1):
        peer = {"ctx": (me + count - distance(j, count)) % count}
        qs.append(pltpu.make_async_remote_copy(
            src_ref=q_ref, dst_ref=q_buf.at[j], send_sem=q_send.at[j], recv_sem=q_recv.at[j],
            device_id=peer, device_id_type=MESH,
        ))
        ls.append(pltpu.make_async_remote_copy(
            src_ref=len_out, dst_ref=len_buf.at[j], send_sem=l_send.at[j], recv_sem=l_recv.at[j],
            device_id=peer, device_id_type=MESH,
        ))
    for copy in kv:
        copy.start()
    for a, b in zip(qs, ls):
        a.start()
        b.start()

    diff = owner_ref[0] - rep
    keep = 1 - diff * diff
    mine = jnp.full((1, width), keep, jnp.int32).astype(jnp.float32).astype(jnp.bfloat16)
    theirs = jnp.full((1, width), 1 - keep, jnp.int32).astype(jnp.float32).astype(jnp.bfloat16)
    locals_[0].wait()
    kv[0].wait_recv()
    k_buf[...] = own_kv[0] * mine + got_kv[0] * theirs
    locals_[1].wait()
    kv[1].wait_recv()
    v_buf[:, :width] = own_kv[1] * mine + got_kv[1] * theirs
    for a, b in zip(qs, ls):
        a.wait_recv()
        b.wait_recv()

    def partial_copy(j):
        return pltpu.make_async_remote_copy(
            src_ref=snd.at[j], dst_ref=rcv.at[j], send_sem=o_send.at[j], recv_sem=o_recv.at[j],
            device_id={"ctx": (me + distance(j, count)) % count}, device_id_type=MESH,
        )

    big = pack * rows
    start = me * span
    lane = lax.broadcasted_iota(jnp.int32, (big, 128), 1)
    first_lane = lax.broadcasted_iota(jnp.int32, (rows, 128), 1) == 0

    def step(g, carry):
        q = q_buf[pl.ds(g * pack, pack)].reshape(big, width)
        lens = len_buf[pl.ds(g * pack, pack)]
        left = jnp.broadcast_to(
            lens.reshape(pack * reqs, 1, 128), (pack * reqs, heads, 128)
        ).reshape(big, 128) - start - lane
        top = jnp.full((big, 128), -1e30, jnp.float32)
        for k in range(span // KEYS):
            s = lax.dot_general(
                q, k_buf[k * KEYS : (k + 1) * KEYS, :], (((1,), (1,)), ((), ())),
                preferred_element_type=jnp.float32,
            )
            for i in range(KEYS // 128):
                at = k * KEYS + i * 128
                part = jnp.where(left > at, s[:, i * 128 : (i + 1) * 128], jnp.float32(-1e30))
                s_buf[:, at : at + 128] = part
                top = jnp.maximum(top, part)
        top = jnp.max(top, axis=1, keepdims=True)
        acc = None
        for k in range(span // DEPTH):
            at = k * DEPTH
            w = jnp.exp2((s_buf[:, at : at + DEPTH] - top) * factor).astype(jnp.bfloat16)
            term = jnp.dot(w, v_buf[at : at + DEPTH, :], preferred_element_type=jnp.float32)
            acc = term if acc is None else acc + term
        for i in range(pack):
            j = g * pack + i
            here = acc[i * rows : (i + 1) * rows]
            stats = jnp.where(first_lane, top[i * rows : (i + 1) * rows], here[:, width:])
            snd[j, :rows, :] = here[:, :width]
            snd[j, rows:, :] = jnp.transpose(stats)[:8]

            @pl.when(j < count - 1)
            def _():
                partial_copy(j).start()

        return carry

    lax.fori_loop(0, count // pack, step, 0)

    for copy in kv:
        copy.wait_send()
    for a, b in zip(qs, ls):
        a.wait_send()
        b.wait_send()
    copies = [partial_copy(j) for j in range(count - 1)]
    for copy in copies:
        copy.wait_recv()
    slots = [rcv.at[j] for j in range(count - 1)] + [snd.at[count - 1]]
    tops, totals = [], []
    for slot in slots:
        turned = jnp.transpose(slot[rows:, :])
        tops.append(turned[:, 0:1])
        totals.append(turned[:, 1:2])
    top = functools.reduce(jnp.maximum, tops)
    total = jnp.zeros((rows, 1), jnp.float32)
    value = jnp.zeros((rows, width), jnp.float32)
    for slot, t, l in zip(slots, tops, totals):
        e = jnp.exp2((t - top) * factor)
        total = total + e * l
        value = value + e * slot[:rows, :]
    out_ref[...] = (value / total).astype(jnp.bfloat16)
    for copy in copies:
        copy.wait_send()


def per_device(queries, cache, owner, lengths):
    count = lax.axis_size("ctx")
    req, heads, width = queries.shape
    rows = req * heads
    span = cache.shape[2]
    pack = 2
    big = pack * rows
    vmem = pl.BlockSpec(memory_space=pltpu.VMEM)
    smem = pl.BlockSpec(memory_space=pltpu.SMEM)
    dma = pltpu.SemaphoreType.DMA
    out = pl.pallas_call(
        functools.partial(kernel, count, heads, pack),
        out_shape=jax.ShapeDtypeStruct((rows, width), jnp.bfloat16),
        in_specs=[vmem, pl.BlockSpec(memory_space=pl.ANY), smem, smem],
        out_specs=vmem,
        scratch_shapes=[
            pltpu.VMEM((2, span, width), jnp.bfloat16),
            pltpu.VMEM((2, span, width), jnp.bfloat16),
            pltpu.VMEM((span, width), jnp.bfloat16),
            pltpu.VMEM((span, 2 * width), jnp.bfloat16),
            pltpu.VMEM((count, rows, width), jnp.bfloat16),
            pltpu.VMEM((count, req, 128), jnp.int32),
            pltpu.VMEM((req, 128), jnp.int32),
            pltpu.VMEM((big, span), jnp.float32),
            pltpu.VMEM((count, rows + 8, width), jnp.float32),
            pltpu.VMEM((count, rows + 8, width), jnp.float32),
            dma((2,)), dma((2,)), dma((2,)),
            dma((count - 1,)), dma((count - 1,)),
            dma((count - 1,)), dma((count - 1,)),
            dma((count - 1,)), dma((count - 1,)),
        ],
        compiler_params=pltpu.CompilerParams(
            collective_id=0, has_side_effects=True, vmem_limit_bytes=48 * 1024 * 1024
        ),
    )(queries.reshape(rows, width), cache, owner, lengths)
    return out.reshape(req, heads, width)


def solution(mesh):
    placed = (
        P(("groups", "ctx", "rep"), None, None),
        P("rep", None, ("groups", "ctx"), None),
        P(("groups", "ctx")),
        P(("groups", "ctx", "rep")),
    )
    return jax.shard_map(
        per_device,
        mesh=mesh,
        in_specs=placed,
        out_specs=P(("groups", "ctx", "rep"), None, None),
        check_vma=False,
    )
```

```python
import functools
import math

import jax
import jax.numpy as jnp
from jax import lax
from jax.experimental import pallas as pl
from jax.experimental.pallas import tpu as pltpu
from jax.sharding import PartitionSpec as P

MESH = pl.DeviceIdType.MESH
KEYS = 256
DEPTH = 1024


def distance(slot, count):
    return count // 2 + (1 - 2 * (slot % 2)) * ((slot + 1) // 2)


def kernel(
    count, heads, pack,
    q_ref, cache_ref, owner_hbm, len_hbm, out_ref,
    own_kv, got_kv, k_buf, v_buf, q_buf, len_buf, len_out, s_buf, snd, mid, rcv,
    owner_ref, len_ref, kv_send, kv_recv, kv_local, q_send, q_recv, l_send, l_recv, o_send, o_recv,
):
    me = lax.axis_index("ctx")
    rep = lax.axis_index("rep")
    rows, width = q_ref.shape
    reqs = rows // heads
    span = cache_ref.shape[2]
    factor = width ** (-0.5) * math.log2(math.e)
    other = 1 - rep
    half = count // 2
    outer, inner = me // 2, me % 2
    beside = outer * 2 + 1 - inner

    def shifted(d, parity):
        return ((outer + half + d) % half) * 2 + parity

    locals_ = [
        pltpu.make_async_copy(cache_ref.at[0, i], own_kv.at[i], kv_local.at[i]) for i in range(2)
    ]
    small = [
        pltpu.make_async_copy(len_hbm, len_ref, kv_local.at[2]),
        pltpu.make_async_copy(owner_hbm, owner_ref, kv_local.at[3]),
        pltpu.make_async_copy(q_ref, q_buf.at[count - 1], kv_local.at[4]),
    ]
    for copy in small + locals_:
        copy.start()

    barrier = pltpu.get_barrier_semaphore()
    for t in range(1, count):
        pl.semaphore_signal(
            barrier, inc=1, device_id={"ctx": (me + t) % count}, device_id_type=MESH
        )
    pl.semaphore_signal(barrier, inc=1, device_id={"rep": other}, device_id_type=MESH)

    for copy in small:
        copy.wait()
    for i in range(reqs):
        len_out[i : i + 1, :] = jnp.full((1, 128), len_ref[i], jnp.int32)
    len_buf[count - 1] = len_out[...]
    v_buf[:, width:] = jnp.ones((span, width), jnp.bfloat16)
    pl.semaphore_wait(barrier, count)

    kv = [
        pltpu.make_async_remote_copy(
            src_ref=cache_ref.at[0, i], dst_ref=got_kv.at[i],
            send_sem=kv_send.at[i], recv_sem=kv_recv.at[i],
            device_id={"rep": other}, device_id_type=MESH,
        )
        for i in range(2)
    ]
    qs, forwards, ls = [], [], []
    for j in range(count - 1):
        d = distance(j % half, half)
        parity = 1 - inner if j < half else inner
        ls.append(pltpu.make_async_remote_copy(
            src_ref=len_out, dst_ref=len_buf.at[j], send_sem=l_send.at[j], recv_sem=l_recv.at[j],
            device_id={"ctx": shifted(-d, parity)}, device_id_type=MESH,
        ))
        if j >= half:
            qs.append(pltpu.make_async_remote_copy(
                src_ref=q_ref, dst_ref=q_buf.at[j],
                send_sem=q_send.at[j], recv_sem=q_recv.at[j],
                device_id={"ctx": shifted(-d, inner)}, device_id_type=MESH,
            ))
    for i in range(half):
        forwards.append(pltpu.make_async_remote_copy(
            src_ref=q_buf.at[half + i], dst_ref=q_buf.at[i],
            send_sem=q_send.at[i], recv_sem=q_recv.at[i],
            device_id={"ctx": beside}, device_id_type=MESH,
        ))
    for copy in kv:
        copy.start()
    for copy in qs + ls + forwards[half - 1 :]:
        copy.start()
    for i in list(range(1, half - 1)) + [0]:
        qs[i].wait_recv()
        forwards[i].start()

    diff = owner_ref[0] - rep
    keep = 1 - diff * diff
    mine = jnp.full((1, width), keep, jnp.int32).astype(jnp.float32).astype(jnp.bfloat16)
    theirs = jnp.full((1, width), 1 - keep, jnp.int32).astype(jnp.float32).astype(jnp.bfloat16)
    locals_[0].wait()
    kv[0].wait_recv()
    k_buf[...] = own_kv[0] * mine + got_kv[0] * theirs
    locals_[1].wait()
    kv[1].wait_recv()
    v_buf[:, :width] = own_kv[1] * mine + got_kv[1] * theirs
    for copy in forwards + ls:
        copy.wait_recv()

    def pair_copy(i):
        return pltpu.make_async_remote_copy(
            src_ref=snd.at[i], dst_ref=mid.at[i], send_sem=o_send.at[i], recv_sem=o_recv.at[i],
            device_id={"ctx": beside}, device_id_type=MESH,
        )

    def final_copy(i):
        j = half + i
        return pltpu.make_async_remote_copy(
            src_ref=snd.at[j], dst_ref=rcv.at[i], send_sem=o_send.at[j], recv_sem=o_recv.at[j],
            device_id={"ctx": shifted(distance(i, half), inner)}, device_id_type=MESH,
        )

    big = pack * rows
    start = me * span
    lane = lax.broadcasted_iota(jnp.int32, (big, 128), 1)
    first_lane = lax.broadcasted_iota(jnp.int32, (rows, 128), 1) == 0

    def partials(g):
        q = q_buf[pl.ds(g * pack, pack)].reshape(big, width)
        lens = len_buf[pl.ds(g * pack, pack)]
        left = jnp.broadcast_to(
            lens.reshape(pack * reqs, 1, 128), (pack * reqs, heads, 128)
        ).reshape(big, 128) - start - lane
        top = jnp.full((big, 128), -1e30, jnp.float32)
        for k in range(span // KEYS):
            s = lax.dot_general(
                q, k_buf[k * KEYS : (k + 1) * KEYS, :], (((1,), (1,)), ((), ())),
                preferred_element_type=jnp.float32,
            )
            for i in range(KEYS // 128):
                at = k * KEYS + i * 128
                part = jnp.where(left > at, s[:, i * 128 : (i + 1) * 128], jnp.float32(-1e30))
                s_buf[:, at : at + 128] = part
                top = jnp.maximum(top, part)
        top = jnp.max(top, axis=1, keepdims=True)
        acc = None
        for k in range(span // DEPTH):
            at = k * DEPTH
            w = jnp.exp2((s_buf[:, at : at + DEPTH] - top) * factor).astype(jnp.bfloat16)
            term = jnp.dot(w, v_buf[at : at + DEPTH, :], preferred_element_type=jnp.float32)
            acc = term if acc is None else acc + term
        return [(top[i * rows : (i + 1) * rows], acc[i * rows : (i + 1) * rows]) for i in range(pack)]

    def put(j, top, total, value):
        snd[j, :rows, :] = value
        snd[j, rows:, :] = jnp.transpose(jnp.where(first_lane, top, total))[:8]

    def first(g, carry):
        for i, (top, acc) in enumerate(partials(g)):
            j = g * pack + i
            put(j, top, acc[:, width:], acc[:, :width])
            pair_copy(j).start()
        return carry

    def second(g, carry):
        for i, (top, acc) in enumerate(partials(half // pack + g)):
            j = g * pack + i
            pair_copy(j).wait_recv()
            turned = jnp.transpose(mid[j, rows:, :])
            best = jnp.maximum(top, turned[:, 0:1])
            here = jnp.exp2((top - best) * factor)
            there = jnp.exp2((turned[:, 0:1] - best) * factor)
            put(
                half + j,
                best,
                acc[:, width:] * here + turned[:, 1:2] * there,
                acc[:, :width] * here + mid[j, :rows, :] * there,
            )

            @pl.when(j < half - 1)
            def _():
                final_copy(j).start()

        return carry

    lax.fori_loop(0, half // pack, first, 0)
    lax.fori_loop(0, half // pack, second, 0)

    for copy in kv + qs + ls + forwards:
        copy.wait_send()
    for i in range(half):
        pair_copy(i).wait_send()
    copies = [final_copy(i) for i in range(half - 1)]
    for copy in copies:
        copy.wait_recv()
    slots = [rcv.at[i] for i in range(half - 1)] + [snd.at[count - 1]]
    tops, totals = [], []
    for slot in slots:
        turned = jnp.transpose(slot[rows:, :])
        tops.append(turned[:, 0:1])
        totals.append(turned[:, 1:2])
    top = functools.reduce(jnp.maximum, tops)
    total = jnp.zeros((rows, 1), jnp.float32)
    value = jnp.zeros((rows, width), jnp.float32)
    for slot, t, l in zip(slots, tops, totals):
        e = jnp.exp2((t - top) * factor)
        total = total + e * l
        value = value + e * slot[:rows, :]
    out_ref[...] = (value / total).astype(jnp.bfloat16)
    for copy in copies:
        copy.wait_send()


def per_device(queries, cache, owner, lengths):
    count = lax.axis_size("ctx")
    req, heads, width = queries.shape
    rows = req * heads
    span = cache.shape[2]
    pack = 2
    big = pack * rows
    vmem = pl.BlockSpec(memory_space=pltpu.VMEM)
    hbm = pl.BlockSpec(memory_space=pltpu.HBM)
    dma = pltpu.SemaphoreType.DMA
    out = pl.pallas_call(
        functools.partial(kernel, count, heads, pack),
        out_shape=jax.ShapeDtypeStruct((rows, width), jnp.bfloat16),
        in_specs=[hbm] * 4,
        out_specs=vmem,
        scratch_shapes=[
            pltpu.VMEM((2, span, width), jnp.bfloat16),
            pltpu.VMEM((2, span, width), jnp.bfloat16),
            pltpu.VMEM((span, width), jnp.bfloat16),
            pltpu.VMEM((span, 2 * width), jnp.bfloat16),
            pltpu.VMEM((count, rows, width), jnp.bfloat16),
            pltpu.VMEM((count, req, 128), jnp.int32),
            pltpu.VMEM((req, 128), jnp.int32),
            pltpu.VMEM((big, span), jnp.float32),
            pltpu.VMEM((count, rows + 8, width), jnp.float32),
            pltpu.VMEM((count // 2, rows + 8, width), jnp.float32),
            pltpu.VMEM((count // 2, rows + 8, width), jnp.float32),
            pltpu.SMEM((1,), jnp.int32),
            pltpu.SMEM((req,), jnp.int32),
            dma((2,)), dma((2,)), dma((5,)),
            dma((count - 1,)), dma((count - 1,)),
            dma((count - 1,)), dma((count - 1,)),
            dma((count - 1,)), dma((count - 1,)),
        ],
        compiler_params=pltpu.CompilerParams(
            collective_id=0, has_side_effects=True, vmem_limit_bytes=63 * 1024 * 1024
        ),
    )(queries.reshape(rows, width), cache, owner, lengths)
    return out.reshape(req, heads, width)


def solution(mesh):
    placed = (
        P(("groups", "ctx", "rep"), None, None),
        P("rep", None, ("groups", "ctx"), None),
        P(("groups", "ctx")),
        P(("groups", "ctx", "rep")),
    )
    return jax.shard_map(
        per_device,
        mesh=mesh,
        in_specs=placed,
        out_specs=P(("groups", "ctx", "rep"), None, None),
        check_vma=False,
    )
```

```python
import functools
import math

import jax
import jax.numpy as jnp
from jax import lax
from jax.experimental import pallas as pl
from jax.experimental.pallas import tpu as pltpu
from jax.sharding import PartitionSpec as P

MESH = pl.DeviceIdType.MESH
KEYS = 256
DEPTH = 1024


def distance(slot, count):
    return count // 2 + (1 - 2 * (slot % 2)) * ((slot + 1) // 2)


def kernel(
    count, heads, pack,
    q_ref, cache_ref, owner_hbm, len_hbm, out_ref,
    own_kv, got_kv, k_buf, v_buf, q_buf, len_buf, len_out, s_buf, top_buf, snd, mid, rcv,
    owner_ref, len_ref, kv_send, kv_recv, kv_local, q_send, q_recv, l_send, l_recv, o_send, o_recv,
):
    me = lax.axis_index("ctx")
    rep = lax.axis_index("rep")
    rows, width = q_ref.shape
    reqs = rows // heads
    span = cache_ref.shape[2]
    factor = width ** (-0.5) * math.log2(math.e)
    other = 1 - rep
    half = count // 2
    outer, inner = me // 2, me % 2
    beside = outer * 2 + 1 - inner

    def shifted(d, parity):
        return ((outer + half + d) % half) * 2 + parity

    locals_ = [
        pltpu.make_async_copy(cache_ref.at[0, i], own_kv.at[i], kv_local.at[i]) for i in range(2)
    ]
    small = [
        pltpu.make_async_copy(len_hbm, len_ref, kv_local.at[2]),
        pltpu.make_async_copy(owner_hbm, owner_ref, kv_local.at[3]),
        pltpu.make_async_copy(q_ref, q_buf.at[count - 1], kv_local.at[4]),
    ]
    for copy in small + locals_:
        copy.start()

    barrier = pltpu.get_barrier_semaphore()
    for t in range(1, count):
        pl.semaphore_signal(
            barrier, inc=1, device_id={"ctx": (me + t) % count}, device_id_type=MESH
        )
    pl.semaphore_signal(barrier, inc=1, device_id={"rep": other}, device_id_type=MESH)

    for copy in small:
        copy.wait()
    for i in range(reqs):
        len_out[i : i + 1, :] = jnp.full((1, 128), len_ref[i], jnp.int32)
    len_buf[count - 1] = len_out[...]
    v_buf[:, width:] = jnp.ones((span, width), jnp.bfloat16)
    pl.semaphore_wait(barrier, count)

    kv = [
        pltpu.make_async_remote_copy(
            src_ref=cache_ref.at[0, i], dst_ref=got_kv.at[i],
            send_sem=kv_send.at[i], recv_sem=kv_recv.at[i],
            device_id={"rep": other}, device_id_type=MESH,
        )
        for i in range(2)
    ]
    qs, forwards, ls = [], [], []
    for i in range(half):
        d = distance(i, half)
        targets = [(2 * i, 1 - inner), (2 * i + 1, inner)]
        for j, parity in targets if i < half - 1 else targets[:1]:
            ls.append(pltpu.make_async_remote_copy(
                src_ref=len_out, dst_ref=len_buf.at[j],
                send_sem=l_send.at[j], recv_sem=l_recv.at[j],
                device_id={"ctx": shifted(-d, parity)}, device_id_type=MESH,
            ))
        if i < half - 1:
            qs.append(pltpu.make_async_remote_copy(
                src_ref=q_ref, dst_ref=q_buf.at[2 * i + 1],
                send_sem=q_send.at[2 * i + 1], recv_sem=q_recv.at[2 * i + 1],
                device_id={"ctx": shifted(-d, inner)}, device_id_type=MESH,
            ))
        forwards.append(pltpu.make_async_remote_copy(
            src_ref=q_buf.at[2 * i + 1], dst_ref=q_buf.at[2 * i],
            send_sem=q_send.at[2 * i], recv_sem=q_recv.at[2 * i],
            device_id={"ctx": beside}, device_id_type=MESH,
        ))
    for copy in qs + ls + forwards[half - 1 :] + kv:
        copy.start()
    for i in list(range(1, half - 1)) + [0]:
        qs[i].wait_recv()
        forwards[i].start()

    diff = owner_ref[0] - rep
    keep = 1 - diff * diff
    mine = jnp.full((1, width), keep, jnp.int32).astype(jnp.float32).astype(jnp.bfloat16)
    theirs = jnp.full((1, width), 1 - keep, jnp.int32).astype(jnp.float32).astype(jnp.bfloat16)
    locals_[0].wait()
    kv[0].wait_recv()
    k_buf[...] = own_kv[0] * mine + got_kv[0] * theirs
    for copy in forwards + ls:
        copy.wait_recv()

    def pair_copy(i):
        return pltpu.make_async_remote_copy(
            src_ref=snd.at[2 * i], dst_ref=mid.at[i],
            send_sem=o_send.at[2 * i], recv_sem=o_recv.at[2 * i],
            device_id={"ctx": beside}, device_id_type=MESH,
        )

    def final_copy(i):
        j = 2 * i + 1
        return pltpu.make_async_remote_copy(
            src_ref=snd.at[j], dst_ref=rcv.at[i], send_sem=o_send.at[j], recv_sem=o_recv.at[j],
            device_id={"ctx": shifted(distance(i, half), inner)}, device_id_type=MESH,
        )

    big = pack * rows
    start = me * span
    lane = lax.broadcasted_iota(jnp.int32, (big, 128), 1)
    first_lane = lax.broadcasted_iota(jnp.int32, (rows, 128), 1) == 0

    def scoring(g):
        q = q_buf[pl.ds(g * pack, pack)].reshape(big, width)
        lens = len_buf[pl.ds(g * pack, pack)]
        left = jnp.broadcast_to(
            lens.reshape(pack * reqs, 1, 128), (pack * reqs, heads, 128)
        ).reshape(big, 128) - start - lane
        return q, left

    def score(q, left, top, begin, end):
        for k in range(begin, end, KEYS):
            s = lax.dot_general(
                q, k_buf[k : k + KEYS, :], (((1,), (1,)), ((), ())),
                preferred_element_type=jnp.float32,
            )
            for at in range(k, k + KEYS, 128):
                part = jnp.where(left > at, s[:, at - k : at - k + 128], jnp.float32(-1e30))
                s_buf[:, at : at + 128] = part
                top = jnp.maximum(top, part)
        return top

    def weigh(top, acc, at):
        w = jnp.concatenate(
            [
                jnp.exp2((s_buf[:, i : i + 128] - top) * factor).astype(jnp.bfloat16)
                for i in range(at, at + DEPTH, 128)
            ],
            axis=1,
        )
        term = jnp.dot(w, v_buf[at : at + DEPTH, :], preferred_element_type=jnp.float32)
        return term if acc is None else acc + term

    def spread(top):
        return jnp.broadcast_to(jnp.max(top, axis=1, keepdims=True), (big, 128))

    def put(j, top, total, value):
        snd[j, :rows, :] = value
        snd[j, rows:, :] = jnp.transpose(jnp.where(first_lane, top, total))[:8]

    def ship(g, top, acc):
        for i in range(pack):
            at = slice(i * rows, (i + 1) * rows)
            put(g * pack + i, top[at], acc[at, width:], acc[at, :width])
            if i == 0:
                pair_copy(g).start()

    def merge(g):
        j = 2 * g + 1
        pair_copy(g).wait_recv()
        mine_ = jnp.transpose(snd[j, rows:, :])
        theirs_ = jnp.transpose(mid[g, rows:, :])
        best = jnp.maximum(mine_[:, 0:1], theirs_[:, 0:1])
        here = jnp.exp2((mine_[:, 0:1] - best) * factor)
        there = jnp.exp2((theirs_[:, 0:1] - best) * factor)
        put(
            j, best, mine_[:, 1:2] * here + theirs_[:, 1:2] * there,
            snd[j, :rows, :] * here + mid[g, :rows, :] * there,
        )

    floor = jnp.full((big, 128), -1e30, jnp.float32)
    top_buf[...] = spread(score(*scoring(0), floor, 0, span))
    locals_[1].wait()
    kv[1].wait_recv()
    v_buf[:, :width] = own_kv[1] * mine + got_kv[1] * theirs

    def step(g, carry):
        top, acc, later = top_buf[...], None, floor
        q, left = scoring(g + 1)
        for at in range(0, span, DEPTH):
            acc = weigh(top, acc, at)
            later = score(q, left, later, at, at + DEPTH)
        top_buf[...] = spread(later)
        ship(g, top, acc)

        @pl.when(g > 0)
        def _():
            merge(g - 1)
            final_copy(g - 1).start()

        return carry

    lax.fori_loop(0, half - 1, step, 0)
    top, acc = top_buf[...], None
    for at in range(0, span, DEPTH):
        acc = weigh(top, acc, at)
        if at == span - 2 * DEPTH:
            merge(half - 2)
            final_copy(half - 2).start()
    ship(half - 1, top, acc)
    merge(half - 1)

    for copy in kv + qs + ls + forwards:
        copy.wait_send()
    for i in range(half):
        pair_copy(i).wait_send()
    copies = [final_copy(i) for i in range(half - 1)]
    for copy in copies:
        copy.wait_recv()
    slots = [rcv.at[i] for i in range(half - 1)] + [snd.at[count - 1]]
    tops, totals = [], []
    for slot in slots:
        turned = jnp.transpose(slot[rows:, :])
        tops.append(turned[:, 0:1])
        totals.append(turned[:, 1:2])
    top = functools.reduce(jnp.maximum, tops)
    total = jnp.zeros((rows, 1), jnp.float32)
    value = jnp.zeros((rows, width), jnp.float32)
    for slot, t, l in zip(slots, tops, totals):
        e = jnp.exp2((t - top) * factor)
        total = total + e * l
        value = value + e * slot[:rows, :]
    out_ref[...] = (value / total).astype(jnp.bfloat16)
    for copy in copies:
        copy.wait_send()


def per_device(queries, cache, owner, lengths):
    count = lax.axis_size("ctx")
    req, heads, width = queries.shape
    rows = req * heads
    span = cache.shape[2]
    pack = 2
    big = pack * rows
    vmem = pl.BlockSpec(memory_space=pltpu.VMEM)
    hbm = pl.BlockSpec(memory_space=pltpu.HBM)
    dma = pltpu.SemaphoreType.DMA
    out = pl.pallas_call(
        functools.partial(kernel, count, heads, pack),
        out_shape=jax.ShapeDtypeStruct((rows, width), jnp.bfloat16),
        in_specs=[hbm] * 4,
        out_specs=vmem,
        scratch_shapes=[
            pltpu.VMEM((2, span, width), jnp.bfloat16),
            pltpu.VMEM((2, span, width), jnp.bfloat16),
            pltpu.VMEM((span, width), jnp.bfloat16),
            pltpu.VMEM((span, 2 * width), jnp.bfloat16),
            pltpu.VMEM((count, rows, width), jnp.bfloat16),
            pltpu.VMEM((count, req, 128), jnp.int32),
            pltpu.VMEM((req, 128), jnp.int32),
            pltpu.VMEM((big, span), jnp.float32),
            pltpu.VMEM((big, 128), jnp.float32),
            pltpu.VMEM((count, rows + 8, width), jnp.float32),
            pltpu.VMEM((count // 2, rows + 8, width), jnp.float32),
            pltpu.VMEM((count // 2, rows + 8, width), jnp.float32),
            pltpu.SMEM((1,), jnp.int32),
            pltpu.SMEM((req,), jnp.int32),
            dma((2,)), dma((2,)), dma((5,)),
            dma((count - 1,)), dma((count - 1,)),
            dma((count - 1,)), dma((count - 1,)),
            dma((count - 1,)), dma((count - 1,)),
        ],
        compiler_params=pltpu.CompilerParams(
            collective_id=0, has_side_effects=True, vmem_limit_bytes=63 * 1024 * 1024
        ),
    )(queries.reshape(rows, width), cache, owner, lengths)
    return out.reshape(req, heads, width)


def solution(mesh):
    placed = (
        P(("groups", "ctx", "rep"), None, None),
        P("rep", None, ("groups", "ctx"), None),
        P(("groups", "ctx")),
        P(("groups", "ctx", "rep")),
    )
    return jax.shard_map(
        per_device,
        mesh=mesh,
        in_specs=placed,
        out_specs=P(("groups", "ctx", "rep"), None, None),
        check_vma=False,
    )
```

```python
import functools
import math

import jax
import jax.numpy as jnp
from jax import lax
from jax.experimental import pallas as pl
from jax.experimental.pallas import tpu as pltpu
from jax.sharding import PartitionSpec as P

MESH = pl.DeviceIdType.MESH
KEYS = 256
DEPTH = 1024


def distance(slot, count):
    return count // 2 + (1 - 2 * (slot % 2)) * ((slot + 1) // 2)


def across(i):
    return 2 * i - 1 + 1 // (i + 1)


def along(i, half):
    return min(2 * i + 2, 2 * half - 1) if isinstance(i, int) else 2 * i + 2


def kernel(
    count, heads, pack,
    q_ref, cache_ref, owner_hbm, len_hbm, out_ref,
    own_kv, got_kv, k_buf, v_buf, q_buf, len_buf, len_out, s_buf, top_buf, snd, mid, rcv,
    owner_ref, len_ref, kv_send, kv_recv, kv_local, q_send, q_recv, l_send, l_recv, o_send, o_recv,
):
    me = lax.axis_index("ctx")
    rep = lax.axis_index("rep")
    rows, width = q_ref.shape
    reqs = rows // heads
    span = cache_ref.shape[2]
    factor = width ** (-0.5) * math.log2(math.e)
    other = 1 - rep
    half = count // 2
    outer, inner = me // 2, me % 2
    beside = outer * 2 + 1 - inner

    def shifted(d, parity):
        return ((outer + half + d) % half) * 2 + parity

    locals_ = [
        pltpu.make_async_copy(cache_ref.at[0, i], own_kv.at[i], kv_local.at[i]) for i in range(2)
    ]
    small = [
        pltpu.make_async_copy(len_hbm, len_ref, kv_local.at[2]),
        pltpu.make_async_copy(owner_hbm, owner_ref, kv_local.at[3]),
        pltpu.make_async_copy(q_ref, q_buf.at[count - 1], kv_local.at[4]),
    ]
    for copy in small + locals_:
        copy.start()

    barrier = pltpu.get_barrier_semaphore()
    for t in range(1, count):
        pl.semaphore_signal(
            barrier, inc=1, device_id={"ctx": (me + t) % count}, device_id_type=MESH
        )
    pl.semaphore_signal(barrier, inc=1, device_id={"rep": other}, device_id_type=MESH)

    for copy in small:
        copy.wait()
    for i in range(reqs):
        len_out[i : i + 1, :] = jnp.full((1, 128), len_ref[i], jnp.int32)
    len_buf[count - 1] = len_out[...]
    v_buf[:, width:] = jnp.ones((span, width), jnp.bfloat16)
    pl.semaphore_wait(barrier, count)

    kv = [
        pltpu.make_async_remote_copy(
            src_ref=cache_ref.at[0, i], dst_ref=got_kv.at[i],
            send_sem=kv_send.at[i], recv_sem=kv_recv.at[i],
            device_id={"rep": other}, device_id_type=MESH,
        )
        for i in range(2)
    ]
    qs, forwards, ls = [], [], []
    for i in range(half):
        d = distance(i, half)
        targets = [(across(i), 1 - inner), (along(i, half), inner)]
        for j, parity in targets if i < half - 1 else targets[:1]:
            ls.append(pltpu.make_async_remote_copy(
                src_ref=len_out, dst_ref=len_buf.at[j],
                send_sem=l_send.at[j], recv_sem=l_recv.at[j],
                device_id={"ctx": shifted(-d, parity)}, device_id_type=MESH,
            ))
        if i < half - 1:
            qs.append(pltpu.make_async_remote_copy(
                src_ref=q_ref, dst_ref=q_buf.at[along(i, half)],
                send_sem=q_send.at[along(i, half)], recv_sem=q_recv.at[along(i, half)],
                device_id={"ctx": shifted(-d, inner)}, device_id_type=MESH,
            ))
        forwards.append(pltpu.make_async_remote_copy(
            src_ref=q_buf.at[along(i, half)], dst_ref=q_buf.at[across(i)],
            send_sem=q_send.at[across(i)], recv_sem=q_recv.at[across(i)],
            device_id={"ctx": beside}, device_id_type=MESH,
        ))
    for copy in qs + ls + forwards[half - 1 :] + kv:
        copy.start()
    for i in list(range(1, half - 1)) + [0]:
        qs[i].wait_recv()
        forwards[i].start()

    diff = owner_ref[0] - rep
    keep = 1 - diff * diff
    mine = jnp.full((1, width), keep, jnp.int32).astype(jnp.float32).astype(jnp.bfloat16)
    theirs = jnp.full((1, width), 1 - keep, jnp.int32).astype(jnp.float32).astype(jnp.bfloat16)
    locals_[0].wait()
    kv[0].wait_recv()
    k_buf[...] = own_kv[0] * mine + got_kv[0] * theirs
    for copy in forwards + ls:
        copy.wait_recv()

    def pair_copy(i):
        return pltpu.make_async_remote_copy(
            src_ref=snd.at[across(i)], dst_ref=mid.at[i],
            send_sem=o_send.at[i], recv_sem=o_recv.at[i],
            device_id={"ctx": beside}, device_id_type=MESH,
        )

    def final_copy(i):
        j = along(i, half)
        return pltpu.make_async_remote_copy(
            src_ref=snd.at[j], dst_ref=rcv.at[i], send_sem=o_send.at[half + i], recv_sem=o_recv.at[half + i],
            device_id={"ctx": shifted(distance(i, half), inner)}, device_id_type=MESH,
        )

    big = pack * rows
    start = me * span
    lane = lax.broadcasted_iota(jnp.int32, (big, 128), 1)
    first_lane = lax.broadcasted_iota(jnp.int32, (rows, 128), 1) == 0

    def scoring(g):
        q = q_buf[pl.ds(g * pack, pack)].reshape(big, width)
        lens = len_buf[pl.ds(g * pack, pack)]
        left = jnp.broadcast_to(
            lens.reshape(pack * reqs, 1, 128), (pack * reqs, heads, 128)
        ).reshape(big, 128) - start - lane
        return q, left

    def score(q, left, top, begin, end):
        for k in range(begin, end, KEYS):
            s = lax.dot_general(
                q, k_buf[k : k + KEYS, :], (((1,), (1,)), ((), ())),
                preferred_element_type=jnp.float32,
            )
            for at in range(k, k + KEYS, 128):
                part = jnp.where(left > at, s[:, at - k : at - k + 128], jnp.float32(-1e30))
                s_buf[:, at : at + 128] = part
                top = jnp.maximum(top, part)
        return top

    def weigh(top, acc, at):
        w = jnp.concatenate(
            [
                jnp.exp2((s_buf[:, i : i + 128] - top) * factor).astype(jnp.bfloat16)
                for i in range(at, at + DEPTH, 128)
            ],
            axis=1,
        )
        term = jnp.dot(w, v_buf[at : at + DEPTH, :], preferred_element_type=jnp.float32)
        return term if acc is None else acc + term

    def spread(top):
        return jnp.broadcast_to(jnp.max(top, axis=1, keepdims=True), (big, 128))

    def put(j, top, total, value):
        snd[j, :rows, :] = value
        snd[j, rows:, :] = jnp.transpose(jnp.where(first_lane, top, total))[:8]

    def rows_of(i, top, acc):
        at = slice(i * rows, (i + 1) * rows)
        return top[at], acc[at, width:], acc[at, :width]

    def cross(i, top, total, value):
        put(across(i), top, total, value)
        pair_copy(i).start()

    def merge(i, top, total, value):
        pair_copy(i).wait_recv()
        turned = jnp.transpose(mid[i, rows:, :])
        best = jnp.maximum(top, turned[:, 0:1])
        here = jnp.exp2((top - best) * factor)
        there = jnp.exp2((turned[:, 0:1] - best) * factor)
        put(
            along(i, half), best, total * here + turned[:, 1:2] * there,
            value * here + mid[i, :rows, :] * there,
        )

    floor = jnp.full((big, 128), -1e30, jnp.float32)
    top_buf[...] = spread(score(*scoring(0), floor, 0, span))
    locals_[1].wait()
    kv[1].wait_recv()
    v_buf[:, :width] = own_kv[1] * mine + got_kv[1] * theirs

    def both(g):
        top, acc, later = top_buf[...], None, floor
        q, left = scoring(g + 1)
        for at in range(0, span, DEPTH):
            acc = weigh(top, acc, at)
            later = score(q, left, later, at, at + DEPTH)
        top_buf[...] = spread(later)
        return top, acc

    def step(g, carry):
        top, acc = both(g)
        cross(g + 1, *rows_of(1, top, acc))
        merge(g - 1, *rows_of(0, top, acc))
        final_copy(g - 1).start()
        return carry

    top, acc = both(0)
    cross(0, *rows_of(0, top, acc))
    cross(1, *rows_of(1, top, acc))
    lax.fori_loop(1, half - 1, step, 0)
    top, acc = top_buf[...], None
    for at in range(0, span, DEPTH):
        acc = weigh(top, acc, at)
    merge(half - 2, *rows_of(0, top, acc))
    final_copy(half - 2).start()
    merge(half - 1, *rows_of(1, top, acc))

    for copy in kv + qs + ls + forwards:
        copy.wait_send()
    for i in range(half):
        pair_copy(i).wait_send()
    copies = [final_copy(i) for i in range(half - 1)]
    for copy in copies:
        copy.wait_recv()
    slots = [rcv.at[i] for i in range(half - 1)] + [snd.at[count - 1]]
    tops, totals = [], []
    for slot in slots:
        turned = jnp.transpose(slot[rows:, :])
        tops.append(turned[:, 0:1])
        totals.append(turned[:, 1:2])
    top = functools.reduce(jnp.maximum, tops)
    total = jnp.zeros((rows, 1), jnp.float32)
    value = jnp.zeros((rows, width), jnp.float32)
    for slot, t, l in zip(slots, tops, totals):
        e = jnp.exp2((t - top) * factor)
        total = total + e * l
        value = value + e * slot[:rows, :]
    out_ref[...] = (value / total).astype(jnp.bfloat16)
    for copy in copies:
        copy.wait_send()


def per_device(queries, cache, owner, lengths):
    count = lax.axis_size("ctx")
    req, heads, width = queries.shape
    rows = req * heads
    span = cache.shape[2]
    pack = 2
    big = pack * rows
    vmem = pl.BlockSpec(memory_space=pltpu.VMEM)
    hbm = pl.BlockSpec(memory_space=pltpu.HBM)
    dma = pltpu.SemaphoreType.DMA
    out = pl.pallas_call(
        functools.partial(kernel, count, heads, pack),
        out_shape=jax.ShapeDtypeStruct((rows, width), jnp.bfloat16),
        in_specs=[hbm] * 4,
        out_specs=vmem,
        scratch_shapes=[
            pltpu.VMEM((2, span, width), jnp.bfloat16),
            pltpu.VMEM((2, span, width), jnp.bfloat16),
            pltpu.VMEM((span, width), jnp.bfloat16),
            pltpu.VMEM((span, 2 * width), jnp.bfloat16),
            pltpu.VMEM((count, rows, width), jnp.bfloat16),
            pltpu.VMEM((count, req, 128), jnp.int32),
            pltpu.VMEM((req, 128), jnp.int32),
            pltpu.VMEM((big, span), jnp.float32),
            pltpu.VMEM((big, 128), jnp.float32),
            pltpu.VMEM((count, rows + 8, width), jnp.float32),
            pltpu.VMEM((count // 2, rows + 8, width), jnp.float32),
            pltpu.VMEM((count // 2, rows + 8, width), jnp.float32),
            pltpu.SMEM((1,), jnp.int32),
            pltpu.SMEM((req,), jnp.int32),
            dma((2,)), dma((2,)), dma((5,)),
            dma((count - 1,)), dma((count - 1,)),
            dma((count - 1,)), dma((count - 1,)),
            dma((count - 1,)), dma((count - 1,)),
        ],
        compiler_params=pltpu.CompilerParams(
            collective_id=0, has_side_effects=True, vmem_limit_bytes=63 * 1024 * 1024
        ),
    )(queries.reshape(rows, width), cache, owner, lengths)
    return out.reshape(req, heads, width)


def solution(mesh):
    placed = (
        P(("groups", "ctx", "rep"), None, None),
        P("rep", None, ("groups", "ctx"), None),
        P(("groups", "ctx")),
        P(("groups", "ctx", "rep")),
    )
    return jax.shard_map(
        per_device,
        mesh=mesh,
        in_specs=placed,
        out_specs=P(("groups", "ctx", "rep"), None, None),
        check_vma=False,
    )
```

```python
import functools
import math

import jax
import jax.numpy as jnp
from jax import lax
from jax.experimental import pallas as pl
from jax.experimental.pallas import tpu as pltpu
from jax.sharding import PartitionSpec as P

MESH = pl.DeviceIdType.MESH
KEYS = 256
DEPTH = 1024


def distance(slot, count):
    return count // 2 + (1 - 2 * (slot % 2)) * ((slot + 1) // 2)


def across(i):
    return 2 * i - 1 + 1 // (i + 1)


def along(i, half):
    return min(2 * i + 2, 2 * half - 1) if isinstance(i, int) else 2 * i + 2


def kernel(
    count, heads, pack,
    q_ref, cache_ref, owner_hbm, len_hbm, out_ref,
    own_kv, got_kv, k_buf, v_buf, q_buf, len_buf, len_out, s_buf, top_buf, snd, mid, rcv,
    owner_ref, len_ref, kv_send, kv_recv, kv_local, q_send, q_recv, l_send, l_recv, o_send, o_recv,
):
    me = lax.axis_index("ctx")
    rep = lax.axis_index("rep")
    rows, width = q_ref.shape
    reqs = rows // heads
    span = cache_ref.shape[2]
    factor = width ** (-0.5) * math.log2(math.e)
    other = 1 - rep
    half = count // 2
    outer, inner = me // 2, me % 2
    beside = outer * 2 + 1 - inner

    def shifted(d, parity):
        return ((outer + half + d) % half) * 2 + parity

    locals_ = [
        pltpu.make_async_copy(cache_ref.at[0, i], own_kv.at[i], kv_local.at[i]) for i in range(2)
    ]
    small = [
        pltpu.make_async_copy(len_hbm, len_ref, kv_local.at[2]),
        pltpu.make_async_copy(owner_hbm, owner_ref, kv_local.at[3]),
        pltpu.make_async_copy(q_ref, q_buf.at[count - 1], kv_local.at[4]),
    ]
    for copy in small + locals_:
        copy.start()

    barrier = pltpu.get_barrier_semaphore()
    for t in range(1, count):
        pl.semaphore_signal(
            barrier, inc=1, device_id={"ctx": (me + t) % count}, device_id_type=MESH
        )
    pl.semaphore_signal(barrier, inc=1, device_id={"rep": other}, device_id_type=MESH)

    for copy in small:
        copy.wait()
    for i in range(reqs):
        len_out[i : i + 1, :] = jnp.full((1, 128), len_ref[i], jnp.int32)
    len_buf[count - 1] = len_out[...]
    v_buf[:, width:] = jnp.ones((span, width), jnp.bfloat16)
    pl.semaphore_wait(barrier, count)

    kv = [
        pltpu.make_async_remote_copy(
            src_ref=cache_ref.at[0, i], dst_ref=got_kv.at[i],
            send_sem=kv_send.at[i], recv_sem=kv_recv.at[i],
            device_id={"rep": other}, device_id_type=MESH,
        )
        for i in range(2)
    ]
    qs, forwards, ls = [], [], []
    for i in range(half):
        d = distance(i, half)
        targets = [(across(i), 1 - inner), (along(i, half), inner)]
        for j, parity in targets if i < half - 1 else targets[:1]:
            ls.append(pltpu.make_async_remote_copy(
                src_ref=len_out, dst_ref=len_buf.at[j],
                send_sem=l_send.at[j], recv_sem=l_recv.at[j],
                device_id={"ctx": shifted(-d, parity)}, device_id_type=MESH,
            ))
        if i < half - 1:
            qs.append(pltpu.make_async_remote_copy(
                src_ref=q_ref, dst_ref=q_buf.at[along(i, half)],
                send_sem=q_send.at[along(i, half)], recv_sem=q_recv.at[along(i, half)],
                device_id={"ctx": shifted(-d, inner)}, device_id_type=MESH,
            ))
        forwards.append(pltpu.make_async_remote_copy(
            src_ref=q_buf.at[along(i, half)], dst_ref=q_buf.at[across(i)],
            send_sem=q_send.at[across(i)], recv_sem=q_recv.at[across(i)],
            device_id={"ctx": beside}, device_id_type=MESH,
        ))
    for copy in qs + ls + forwards[half - 1 :] + kv:
        copy.start()
    for i in list(range(1, half - 1)) + [0]:
        qs[i].wait_recv()
        forwards[i].start()

    diff = owner_ref[0] - rep
    keep = 1 - diff * diff
    mine = jnp.full((1, width), keep, jnp.int32).astype(jnp.float32).astype(jnp.bfloat16)
    theirs = jnp.full((1, width), 1 - keep, jnp.int32).astype(jnp.float32).astype(jnp.bfloat16)
    locals_[0].wait()
    kv[0].wait_recv()
    k_buf[...] = own_kv[0] * mine + got_kv[0] * theirs
    for copy in forwards[:2] + [ls[0], ls[2]]:
        copy.wait_recv()

    def pair_copy(i):
        return pltpu.make_async_remote_copy(
            src_ref=snd.at[across(i)], dst_ref=mid.at[i],
            send_sem=o_send.at[i], recv_sem=o_recv.at[i],
            device_id={"ctx": beside}, device_id_type=MESH,
        )

    def final_copy(i):
        j = along(i, half)
        return pltpu.make_async_remote_copy(
            src_ref=snd.at[j], dst_ref=rcv.at[i], send_sem=o_send.at[half + i], recv_sem=o_recv.at[half + i],
            device_id={"ctx": shifted(distance(i, half), inner)}, device_id_type=MESH,
        )

    big = pack * rows
    start = me * span
    lane = lax.broadcasted_iota(jnp.int32, (big, 128), 1)
    first_lane = lax.broadcasted_iota(jnp.int32, (rows, 128), 1) == 0

    def scoring(g):
        q = q_buf[pl.ds(g * pack, pack)].reshape(big, width)
        lens = len_buf[pl.ds(g * pack, pack)]
        left = jnp.broadcast_to(
            lens.reshape(pack * reqs, 1, 128), (pack * reqs, heads, 128)
        ).reshape(big, 128) - start - lane
        return q, left

    def score(q, left, top, begin, end):
        for k in range(begin, end, KEYS):
            s = lax.dot_general(
                q, k_buf[k : k + KEYS, :], (((1,), (1,)), ((), ())),
                preferred_element_type=jnp.float32,
            )
            for at in range(k, k + KEYS, 128):
                part = jnp.where(left > at, s[:, at - k : at - k + 128], jnp.float32(-1e30))
                s_buf[:, at : at + 128] = part
                top = jnp.maximum(top, part)
        return top

    def weigh(top, acc, at, begin=0, end=big):
        w = jnp.concatenate(
            [
                jnp.exp2((s_buf[begin:end, i : i + 128] - top) * factor).astype(jnp.bfloat16)
                for i in range(at, at + DEPTH, 128)
            ],
            axis=1,
        )
        term = jnp.dot(w, v_buf[at : at + DEPTH, :], preferred_element_type=jnp.float32)
        return term if acc is None else acc + term

    def spread(top):
        return jnp.broadcast_to(jnp.max(top, axis=1, keepdims=True), (big, 128))

    def put(j, top, total, value):
        snd[j, :rows, :] = value
        snd[j, rows:, :] = jnp.transpose(jnp.where(first_lane, top, total))[:8]

    def rows_of(i, top, acc):
        at = slice(i * rows, (i + 1) * rows)
        return top[at], acc[at, width:], acc[at, :width]

    def cross(i, top, total, value):
        put(across(i), top, total, value)
        pair_copy(i).start()

    def merge(i, top, total, value):
        pair_copy(i).wait_recv()
        turned = jnp.transpose(mid[i, rows:, :])
        best = jnp.maximum(top, turned[:, 0:1])
        here = jnp.exp2((top - best) * factor)
        there = jnp.exp2((turned[:, 0:1] - best) * factor)
        put(
            along(i, half), best, total * here + turned[:, 1:2] * there,
            value * here + mid[i, :rows, :] * there,
        )

    floor = jnp.full((big, 128), -1e30, jnp.float32)
    top_buf[...] = spread(score(*scoring(0), floor, 0, span))
    for copy in forwards[2:] + ls[1:2] + ls[3:]:
        copy.wait_recv()
    locals_[1].wait()
    kv[1].wait_recv()
    v_buf[:, :width] = own_kv[1] * mine + got_kv[1] * theirs

    def both(g):
        top, acc, later = top_buf[...], None, floor
        q, left = scoring(g + 1)
        for at in range(0, span, DEPTH):
            acc = weigh(top, acc, at)
            later = score(q, left, later, at, at + DEPTH)
        top_buf[...] = spread(later)
        return top, acc

    def step(g, carry):
        top, acc = both(g)
        cross(g + 1, *rows_of(1, top, acc))
        merge(g - 1, *rows_of(0, top, acc))
        final_copy(g - 1).start()
        return carry

    top, acc = both(0)
    cross(0, *rows_of(0, top, acc))
    cross(1, *rows_of(1, top, acc))
    lax.fori_loop(1, half - 1, step, 0)
    for i in range(pack):
        begin, end = i * rows, (i + 1) * rows
        top, acc = top_buf[begin:end, :], None
        for at in range(0, span, DEPTH):
            acc = weigh(top, acc, at, begin, end)
        merge(half - pack + i, top, acc[:, width:], acc[:, :width])
        if i == 0:
            final_copy(half - 2).start()

    for copy in kv + qs + ls + forwards:
        copy.wait_send()
    for i in range(half):
        pair_copy(i).wait_send()
    copies = [final_copy(i) for i in range(half - 1)]
    for copy in copies:
        copy.wait_recv()
    slots = [rcv.at[i] for i in range(half - 1)] + [snd.at[count - 1]]
    tops, totals = [], []
    for slot in slots:
        turned = jnp.transpose(slot[rows:, :])
        tops.append(turned[:, 0:1])
        totals.append(turned[:, 1:2])
    top = functools.reduce(jnp.maximum, tops)
    total = jnp.zeros((rows, 1), jnp.float32)
    value = jnp.zeros((rows, width), jnp.float32)
    for slot, t, l in zip(slots, tops, totals):
        e = jnp.exp2((t - top) * factor)
        total = total + e * l
        value = value + e * slot[:rows, :]
    out_ref[...] = (value / total).astype(jnp.bfloat16)
    for copy in copies:
        copy.wait_send()


def per_device(queries, cache, owner, lengths):
    count = lax.axis_size("ctx")
    req, heads, width = queries.shape
    rows = req * heads
    span = cache.shape[2]
    pack = 2
    big = pack * rows
    vmem = pl.BlockSpec(memory_space=pltpu.VMEM)
    hbm = pl.BlockSpec(memory_space=pltpu.HBM)
    dma = pltpu.SemaphoreType.DMA
    out = pl.pallas_call(
        functools.partial(kernel, count, heads, pack),
        out_shape=jax.ShapeDtypeStruct((rows, width), jnp.bfloat16),
        in_specs=[hbm] * 4,
        out_specs=vmem,
        scratch_shapes=[
            pltpu.VMEM((2, span, width), jnp.bfloat16),
            pltpu.VMEM((2, span, width), jnp.bfloat16),
            pltpu.VMEM((span, width), jnp.bfloat16),
            pltpu.VMEM((span, 2 * width), jnp.bfloat16),
            pltpu.VMEM((count, rows, width), jnp.bfloat16),
            pltpu.VMEM((count, req, 128), jnp.int32),
            pltpu.VMEM((req, 128), jnp.int32),
            pltpu.VMEM((big, span), jnp.float32),
            pltpu.VMEM((big, 128), jnp.float32),
            pltpu.VMEM((count, rows + 8, width), jnp.float32),
            pltpu.VMEM((count // 2, rows + 8, width), jnp.float32),
            pltpu.VMEM((count // 2, rows + 8, width), jnp.float32),
            pltpu.SMEM((1,), jnp.int32),
            pltpu.SMEM((req,), jnp.int32),
            dma((2,)), dma((2,)), dma((5,)),
            dma((count - 1,)), dma((count - 1,)),
            dma((count - 1,)), dma((count - 1,)),
            dma((count - 1,)), dma((count - 1,)),
        ],
        compiler_params=pltpu.CompilerParams(
            collective_id=0, has_side_effects=True, vmem_limit_bytes=63 * 1024 * 1024
        ),
    )(queries.reshape(rows, width), cache, owner, lengths)
    return out.reshape(req, heads, width)


def solution(mesh):
    placed = (
        P(("groups", "ctx", "rep"), None, None),
        P("rep", None, ("groups", "ctx"), None),
        P(("groups", "ctx")),
        P(("groups", "ctx", "rep")),
    )
    return jax.shard_map(
        per_device,
        mesh=mesh,
        in_specs=placed,
        out_specs=P(("groups", "ctx", "rep"), None, None),
        check_vma=False,
    )
```
